32 devices in a mesh: batch: 4 (over x, core), patch: 8 (over z, y).
Axes of the slice: x: 2, y: 2, z: 4, core: 2. Of those that a mesh axis runs over, the one named last changes fastest.
Arguments:
- features: bfloat16 [24, 512, 1280], P('patch', 'batch'), parts along dimension 1, may hold values from -80 to 80
- stale_kv: bfloat16 [8, 3072, 640], P('batch', 'patch'), parts along dimension 0, may hold values from -260 to 260
- timestep: int32 [4], P('batch'), parts along dimension 0, may hold values from 0 to 999
- time_w: bfloat16 [320, 640], replicated, may hold values from -0.3125 to 0.3125
- gain_one: float32 [1280], replicated, may hold values from 0.5 to 1.5
- conv_w: bfloat16 [3, 3, 1280, 640], replicated, may hold values from -0.0546875 to 0.0546875
- shortcut_w: bfloat16 [1280, 640], replicated, may hold values from -0.078125 to 0.078125
- gain_two: float32 [640], replicated, may hold values from 0.5 to 1.5
- query_w: bfloat16 [640, 640], replicated, may hold values from -0.25 to 0.25
- key_w: bfloat16 [640, 640], replicated, may hold values from -0.5 to 0.5
- value_w: bfloat16 [640, 640], replicated, may hold values from -1 to 1
- out_w: bfloat16 [640, 640], replicated, may hold values from -0.25 to 0.25
Outputs:
- mixed_out: bfloat16 [24, 512, 640], P('patch', 'batch'), parts along dimension 1
The draws below stay inside these ranges and needn't reach their ends.
There are 4 independent parts, one for each index of `batch`. The reference program is written for one: setup_inputs(seed, part) draws one part's arguments, and reference() takes and returns one part's arrays. A program takes and returns all parts, laid end to end along the dimension named above; an argument that names none is the same for every part. Nothing has to cross between parts.
All inputs are finite; a program needn't handle non-finite values.
Results may differ from the reference program's by a relative error of at most 0.014.
Values may be sent and summed in bfloat16 or wider, within the bound.
A program may use at most 192 MiB of HBM per device.

```python
import math
import jax
import jax.numpy as jnp
from jax import lax

ROWS_DEV = 3
COLS = 128
C_IN = 1280
C_OUT = 640
HEAD_DIM = 64
GROUPS = 32
FREQ = 320
HEADS = 10
ROWS = 24
TOKENS = 3072
N_PATCH = 8


def draw_features(key, part):
    key = jax.random.fold_in(key, 11)
    key_base, key_chan = jax.random.split(key, 2)
    rows = jnp.arange(ROWS, dtype=jnp.float32)
    row_scale = 1.0 + 2.0 * rows / max(ROWS - 1, 1)
    chan = jax.random.uniform(key_chan, (C_IN,), jnp.float32, 0.0, 1.0)
    chan_scale = 0.3 * jnp.exp(chan * math.log(10.0))
    base = jnp.clip(jax.random.normal(key_base, (ROWS, COLS, C_IN), jnp.float32), -4.0, 4.0)
    return (base * row_scale[:, None, None] * chan_scale[None, None, :]).astype(jnp.bfloat16)


def draw_stale_kv(key, part):
    key = jax.random.fold_in(key, 23)
    key_base = jax.random.fold_in(key, 0)
    scale = jnp.array([2.0, 4.0], jnp.float32)[:, None, None]
    base = jnp.clip(jax.random.normal(key_base, (2, TOKENS, C_OUT), jnp.float32), -4.0, 4.0)
    return (base * scale).astype(jnp.bfloat16)


def normal_values(rng, dims, scale, most, kind=jnp.bfloat16):
    values = scale * jax.random.normal(rng, dims, jnp.float32)
    return jnp.clip(values, min=-most, max=most).astype(kind)


def setup_inputs(seed: int = 0, part: int = 0) -> dict:
    splits = jax.random.split(jax.random.key(seed), 13)
    own_keys = jax.random.split(jax.random.fold_in(splits[12], part), 13)
    return {
        "features": draw_features(jax.random.fold_in(jax.random.fold_in(splits[12], part), 71), part),
        "stale_kv": draw_stale_kv(jax.random.fold_in(jax.random.fold_in(splits[12], part), 71), part),
        "timestep": jax.random.randint(own_keys[2], (1,), 0, 1000).astype(jnp.int32),
        "time_w": normal_values(splits[3], (FREQ, C_OUT), FREQ ** -0.5, 0.3125),
        "gain_one": jnp.clip(1.0 + 0.1 * jax.random.normal(splits[4], (C_IN,), jnp.float32), 0.5, 1.5),
        "conv_w": normal_values(splits[5], (3, 3, C_IN, C_OUT), (9 * C_IN) ** -0.5, 0.0546875),
        "shortcut_w": normal_values(splits[6], (C_IN, C_OUT), (4 * C_IN) ** -0.5, 0.078125),
        "gain_two": jnp.clip(1.0 + 0.1 * jax.random.normal(splits[7], (C_OUT,), jnp.float32), 0.5, 1.5),
        "query_w": normal_values(splits[8], (C_OUT, C_OUT), C_OUT ** -0.5, 0.25),
        "key_w": normal_values(splits[9], (C_OUT, C_OUT), (C_OUT // 4) ** -0.5, 0.5),
        "value_w": normal_values(splits[10], (C_OUT, C_OUT), (C_OUT // 16) ** -0.5, 1.0),
        "out_w": normal_values(splits[11], (C_OUT, C_OUT), C_OUT ** -0.5, 0.25),
    }


def group_norm(values, gain, eps):
    rows, cols, width = values.shape
    grouped = values.reshape(rows * cols, GROUPS, width // GROUPS)
    center = lax.optimization_barrier(jnp.mean(grouped, axis=(0, 2)))
    offset = grouped - center[None, :, None]
    spread = lax.optimization_barrier(jnp.mean(offset * offset, axis=(0, 2)))
    scaled = offset * lax.rsqrt(spread + eps)[None, :, None]
    return scaled.reshape(rows, cols, width) * gain.astype(jnp.float32)

def reference(features, stale_kv, timestep, time_w, gain_one, conv_w, shortcut_w, gain_two, query_w, key_w, value_w, out_w):
    block = ROWS_DEV * COLS
    act = jax.nn.silu(group_norm(features.astype(jnp.float32), gain_one, 1e-05)).astype(jnp.bfloat16)
    padded = jnp.pad(act, ((1, 1), (1, 1), (0, 0)))
    conv = jnp.zeros((TOKENS, C_OUT), jnp.float32)
    for row_off in range(3):
        for col_off in range(3):
            window = padded[row_off:row_off + ROWS, col_off:col_off + COLS].reshape(TOKENS, C_IN)
            conv = conv + jnp.dot(window, conv_w[row_off, col_off], preferred_element_type=jnp.float32)
    half = FREQ // 2
    freqs = jnp.exp(-math.log(10000.0) * jnp.arange(half, dtype=jnp.float32) / half)
    angles = timestep.astype(jnp.float32)[0] * freqs
    embed = jnp.concatenate([jnp.cos(angles), jnp.sin(angles)]).astype(jnp.bfloat16)
    shift = jnp.dot(embed[None, :], time_w, preferred_element_type=jnp.float32)
    mixed = jnp.dot(features.reshape(TOKENS, C_IN), shortcut_w, preferred_element_type=jnp.float32) + conv + shift
    normed = group_norm(mixed.reshape(ROWS, COLS, C_OUT), gain_two, 1e-06).astype(jnp.bfloat16).reshape(TOKENS, C_OUT)
    queries = jnp.dot(normed, query_w, preferred_element_type=jnp.float32).astype(jnp.bfloat16)
    fresh_keys = jnp.dot(normed, key_w, preferred_element_type=jnp.float32).astype(jnp.bfloat16)
    fresh_values = jnp.dot(normed, value_w, preferred_element_type=jnp.float32).astype(jnp.bfloat16)
    query_blocks = queries.reshape(N_PATCH, block, HEADS, HEAD_DIM)

    def one_block(item):
        index, rows_q = item
        begin = index * block
        zero = jnp.int32(0)
        keys = lax.dynamic_update_slice(stale_kv[0], lax.dynamic_slice(fresh_keys, (begin, zero), (block, C_OUT)), (begin, zero))
        values = lax.dynamic_update_slice(stale_kv[1], lax.dynamic_slice(fresh_values, (begin, zero), (block, C_OUT)), (begin, zero))
        keys = keys.reshape(N_PATCH, block, HEADS, HEAD_DIM).astype(jnp.float32)
        values = values.reshape(N_PATCH, block, HEADS, HEAD_DIM).astype(jnp.float32)
        scores = jnp.einsum('qhd,nkhd->hqnk', rows_q.astype(jnp.float32), keys) * 0.125
        top = lax.optimization_barrier(jnp.max(scores, axis=3, keepdims=True))
        expo = jnp.exp(scores - top)
        total = lax.optimization_barrier(jnp.sum(expo, axis=3))
        weights = expo.astype(jnp.bfloat16).astype(jnp.float32)
        summed = jnp.einsum('hqnk,nkhd->hqnd', weights, values)
        partial_value = lax.optimization_barrier((summed / total[..., None]).astype(jnp.bfloat16)).astype(jnp.float32)
        lse = top[..., 0] + jnp.log(total)
        best = lax.optimization_barrier(jnp.max(lse, axis=2, keepdims=True))
        share = jnp.exp(lse - best)
        result = lax.optimization_barrier(jnp.sum(share[..., None] * partial_value, axis=2)) / lax.optimization_barrier(jnp.sum(share, axis=2))[..., None]
        return jnp.transpose(result, (1, 0, 2)).reshape(block, C_OUT).astype(jnp.bfloat16)
    attended = lax.map(one_block, (jnp.arange(N_PATCH, dtype=jnp.int32), query_blocks)).reshape(TOKENS, C_OUT)
    result = mixed + jnp.dot(attended, out_w, preferred_element_type=jnp.float32)
    return result.astype(jnp.bfloat16).reshape(ROWS, COLS, C_OUT)
```

```python
import functools
import math

import jax
import jax.numpy as jnp
from jax import lax
from jax.experimental import pallas as pl
from jax.experimental.pallas import tpu as pltpu
from jax.sharding import PartitionSpec as P

HEAD_DIM = 64
GROUPS = 32
FREQ = 320
LANES = 128
F32 = jnp.float32
BF16 = jnp.bfloat16
EXP_SCALE = 0.125 * math.log2(math.e)
LN2 = math.log(2.0)
MESH = pl.DeviceIdType.MESH


def dot(a, b):
    return jnp.dot(a, b, preferred_element_type=F32)


def split_dot(a, b):
    high = a.astype(BF16)
    rest = a - high.astype(F32)
    mid = rest.astype(BF16)
    low = (rest - mid.astype(F32)).astype(BF16)
    return dot(high, b) + dot(mid, b) + dot(low, b)


def members(shape, chan_dim, size):
    chan = lax.broadcasted_iota(jnp.int32, shape, chan_dim)
    group = lax.broadcasted_iota(jnp.int32, shape, 1 - chan_dim) * size
    return jnp.where((chan >= group) & (chan < group + size), 1.0, 0.0).astype(BF16)


def two_rows(first, second):
    row = lax.broadcasted_iota(jnp.int32, (8, first.shape[1]), 0)
    return jnp.where(row == 0, first, jnp.where(row == 1, second, 0.0))


def group_stats(total, count, eps):
    width = total.shape[1]
    size = width // GROUPS
    grouped = split_dot(total, members((width, LANES), 0, size))
    center = grouped[0:1] / count
    spread = jnp.maximum(grouped[1:2] / count - center * center, 0.0)
    wide = split_dot(two_rows(center, lax.rsqrt(spread + eps)), members((LANES, width), 1, size))
    return wide[0:1], wide[1:2]


def half_mask(rows):
    return lax.broadcasted_iota(jnp.int32, (rows, LANES), 1) < HEAD_DIM


def scores_of(query, keys):
    return lax.dot_general(query, keys, (((1,), (1,)), ((), ())), preferred_element_type=F32)


def fused_kernel(
    size,
    kv_ref,
    feat_ref,
    embed_ref,
    time_ref,
    gain_one_ref,
    conv_ref,
    short_ref,
    gain_two_ref,
    qw_ref,
    kw_ref,
    vw_ref,
    ow_ref,
    out_ref,
    feat,
    convw,
    shortw,
    projw,
    act,
    parts,
    mixed,
    kvs,
    stat_out1,
    stat_in1,
    stat_out2,
    stat_in2,
    fresh,
    q_in,
    own_val,
    own_lse,
    acc,
    top,
    res,
    res_lse,
    res_in,
    lse_in,
    load_sem,
    conv_sem,
    kv_send,
    kv_recv,
    kv_own,
    stat_send,
    stat_recv,
    halo_send,
    halo_recv,
    q_send,
    q_recv,
    res_send,
    res_recv,
    lse_send,
    lse_recv,
):
    me = lax.axis_index("patch")
    block, width_in = feat.shape
    width = mixed.shape[1]
    pairs = width // LANES
    cols = (act.shape[0] - block) // 2

    loads = [
        pltpu.make_async_copy(feat_ref, feat, load_sem.at[0]),
        pltpu.make_async_copy(short_ref, shortw, load_sem.at[1]),
        pltpu.make_async_copy(qw_ref, projw.at[0], load_sem.at[2]),
        pltpu.make_async_copy(kw_ref, projw.at[1], load_sem.at[3]),
        pltpu.make_async_copy(vw_ref, projw.at[2], load_sem.at[4]),
        pltpu.make_async_copy(ow_ref, projw.at[3], load_sem.at[5]),
    ]
    conv_loads = [
        [
            pltpu.make_async_copy(conv_ref.at[dy, dx], convw.at[dy, dx], conv_sem.at[dy, dx])
            for dx in range(3)
        ]
        for dy in range(3)
    ]
    loads[0].start()
    loads[1].start()
    for dy in (1, 0, 2):
        for dx in range(3):
            conv_loads[dy][dx].start()
    for load in loads[2:]:
        load.start()

    barrier = pltpu.get_barrier_semaphore()

    def greet(step, unused):
        pl.semaphore_signal(
            barrier, inc=1, device_id={"patch": lax.rem(me + step, size)}, device_id_type=MESH
        )
        return unused

    lax.fori_loop(1, size, greet, 0)

    def first_pair(device):
        return lax.div(device * pairs, size)

    def last_pair(device):
        return lax.div(device * pairs + pairs - 1, size)

    def stale(pair):
        return kv_ref.at[:, :, pl.ds(pl.multiple_of(pair * LANES, LANES), LANES)]

    def place(slot, owner):
        return kvs.at[slot, :, pl.ds(pl.multiple_of(owner * block, block), block), :]

    def kv_copy(slot, pair, target, index):
        return pltpu.make_async_remote_copy(
            src_ref=stale(pair),
            dst_ref=place(slot, me),
            send_sem=kv_send.at[slot, target],
            recv_sem=kv_recv.at[slot, index],
            device_id={"patch": target},
            device_id_type=MESH,
        )

    my_first = first_pair(me)
    my_last = last_pair(me)
    own_copies = [
        pltpu.make_async_copy(stale(my_first), place(0, me), kv_own.at[0]),
        pltpu.make_async_copy(stale(my_last), place(1, me), kv_own.at[1]),
    ]
    own_copies[0].start()
    own_copies[1].start()

    loads[0].wait()

    def sum_rows(step, carry):
        first, second = carry
        x = feat[pl.ds(pl.multiple_of(step * 16, 16), 16), :].astype(F32)
        low, high = x[:8], x[8:]
        return first + (low + high), second + (low * low + high * high)

    zero = jnp.zeros((8, width_in), F32)
    first, second = lax.fori_loop(0, block // 16, sum_rows, (zero, zero))
    stat_out1[...] = two_rows(
        jnp.sum(first, axis=0, keepdims=True), jnp.sum(second, axis=0, keepdims=True)
    )
    pl.semaphore_wait(barrier, size - 1)

    def stat_copy(which, out, into, target, index):
        return pltpu.make_async_remote_copy(
            src_ref=out,
            dst_ref=into.at[me],
            send_sem=stat_send.at[which, target],
            recv_sem=stat_recv.at[which, index],
            device_id={"patch": target},
            device_id_type=MESH,
        )

    def stats_start(which, out, into):
        def send(step, unused):
            target = lax.rem(me + step, size)
            stat_copy(which, out, into, target, me).start()
            return unused

        lax.fori_loop(1, size, send, 0)

    def stats_finish(which, out, into):
        def receive(step, total):
            source = lax.rem(me + step, size)
            pltpu.make_async_remote_copy(
                src_ref=out,
                dst_ref=into.at[source],
                send_sem=stat_send.at[which, source],
                recv_sem=stat_recv.at[which, source],
                device_id={"patch": source},
                device_id_type=MESH,
            ).wait()
            return total + into[source]

        return lax.fori_loop(1, size, receive, out[...])

    stats_start(0, stat_out1, stat_in1)

    def send_kv(step, unused):
        target = lax.rem(me + step, size)
        kv_copy(0, first_pair(target), target, me).start()

        @pl.when(last_pair(target) != first_pair(target))
        def _():
            kv_copy(1, last_pair(target), target, me).start()

        return unused

    lax.fori_loop(1, size, send_kv, 0)

    loads[1].wait()
    mixed[...] = dot(feat[...], shortw[...]) + dot(embed_ref[...], time_ref[...])[0:1]

    total = stats_finish(0, stat_out1, stat_in1)
    count = float(size * block * (width_in // GROUPS))
    center, inverse = group_stats(total, count, 1e-05)
    scale = inverse * gain_one_ref[...]

    def activate(step, unused):
        x = feat[pl.ds(pl.multiple_of(step * 16, 16), 16), :].astype(F32)
        y = (x - center) * scale
        half = 0.5 * y
        z = half + half * jnp.tanh(half)
        act[pl.ds(pl.multiple_of(cols + step * 16, 16), 16), :] = z.astype(BF16)
        return unused

    lax.fori_loop(0, block // 16, activate, 0)

    top_row = act.at[pl.ds(cols, cols), :]
    bottom_row = act.at[pl.ds(block, cols), :]
    above = act.at[pl.ds(0, cols), :]
    below = act.at[pl.ds(block + cols, cols), :]
    up = pltpu.make_async_remote_copy(
        src_ref=top_row,
        dst_ref=below,
        send_sem=halo_send.at[0],
        recv_sem=halo_recv.at[0],
        device_id={"patch": lax.rem(me + size - 1, size)},
        device_id_type=MESH,
    )
    down = pltpu.make_async_remote_copy(
        src_ref=bottom_row,
        dst_ref=above,
        send_sem=halo_send.at[1],
        recv_sem=halo_recv.at[1],
        device_id={"patch": lax.rem(me + 1, size)},
        device_id_type=MESH,
    )

    @pl.when(me > 0)
    def _():
        up.start()

    @pl.when(me < size - 1)
    def _():
        down.start()

    @pl.when(me == 0)
    def _():
        above[...] = jnp.zeros((cols, width_in), BF16)

    @pl.when(me == size - 1)
    def _():
        below[...] = jnp.zeros((cols, width_in), BF16)

    for dx in range(3):
        conv_loads[1][dx].wait()

    def middle(dx, unused):
        parts[dx] = dot(act[pl.ds(cols, block), :], convw[1, dx])
        return unused

    lax.fori_loop(0, 3, middle, 0)

    for dy in (0, 2):
        for dx in range(3):
            conv_loads[dy][dx].wait()

    @pl.when(me > 0)
    def _():
        up.wait_send()
        down.wait_recv()

    @pl.when(me < size - 1)
    def _():
        down.wait_send()
        up.wait_recv()

    def outer(dx, unused):
        parts[dx] = (
            parts[dx]
            + dot(act[pl.ds(0, block), :], convw[0, dx])
            + dot(act[pl.ds(2 * cols, block), :], convw[2, dx])
        )
        return unused

    lax.fori_loop(0, 3, outer, 0)

    col = lax.rem(lax.broadcasted_iota(jnp.int32, (block, LANES), 0), cols)
    for pair in range(pairs):
        lanes = pl.ds(pair * LANES, LANES)
        left = jnp.where(col == 0, 0.0, pltpu.roll(parts[0, :, lanes], 1, 0))
        right = jnp.where(col == cols - 1, 0.0, pltpu.roll(parts[2, :, lanes], block - 1, 0))
        value = mixed[:, lanes] + (left + parts[1, :, lanes] + right)
        mixed[:, lanes] = value
        stat_out2[:, lanes] = two_rows(
            jnp.sum(value, axis=0, keepdims=True), jnp.sum(value * value, axis=0, keepdims=True)
        )
    stats_start(1, stat_out2, stat_in2)
    for load in loads[2:]:
        load.wait()
    total = stats_finish(1, stat_out2, stat_in2)
    count = float(size * block * (width // GROUPS))
    center, inverse = group_stats(total, count, 1e-06)
    normed = ((mixed[...] - center) * (inverse * gain_two_ref[...])).astype(BF16)

    def task_of(pair):
        task = pair * size + me
        return lax.div(task, pairs), lax.rem(task, pairs)

    def q_remote(pair, target, slot):
        return pltpu.make_async_remote_copy(
            src_ref=fresh.at[0, pair],
            dst_ref=q_in.at[slot],
            send_sem=q_send.at[pair],
            recv_sem=q_recv.at[slot],
            device_id={"patch": target},
            device_id_type=MESH,
        )

    queries = dot(normed, projw[0]).astype(BF16)
    for pair in range(pairs):
        fresh[0, pair] = queries[:, pair * LANES : (pair + 1) * LANES]
    for pair in range(pairs):
        target, slot = task_of(pair)

        @pl.when(target != me)
        def _():
            q_remote(pair, target, slot).start()

        @pl.when(target == me)
        def _():
            pltpu.make_async_copy(fresh.at[0, pair], q_in.at[slot], q_recv.at[slot]).start()

    for kind in (1, 2):
        value = dot(normed, projw[kind]).astype(BF16)
        for pair in range(pairs):
            fresh[kind, pair] = value[:, pair * LANES : (pair + 1) * LANES]

    left_half = half_mask(block)
    ones = jnp.ones((block, LANES), BF16)

    def heads_of(query):
        none = jnp.zeros_like(query)
        return jnp.where(left_half, query, none), jnp.where(left_half, none, query)

    def finish(pieces):
        values, lses = [], []
        for summed, height in pieces:
            weight = summed[:, LANES:]
            values.append(summed[:, :LANES] / weight)
            lses.append(height * 0.125 + jnp.log(weight))
        return jnp.where(left_half, *values), jnp.where(left_half, *lses)

    def own_attention(pair, unused):
        keys = fresh[1, pair]
        values = jnp.concatenate([fresh[2, pair], ones], axis=1)
        pieces = []
        for query in heads_of(fresh[0, pair]):
            scores = scores_of(query, keys)
            height = jnp.max(scores, axis=1, keepdims=True)
            weights = jnp.exp2((scores - height) * EXP_SCALE).astype(BF16)
            pieces.append((dot(weights, values), jnp.broadcast_to(height, (block, LANES))))
        own_val[pair], own_lse[pair] = finish(pieces)
        return unused

    lax.fori_loop(0, pairs, own_attention, 0)

    own_copies[0].wait()
    own_copies[1].wait()

    def kv_wait(slot, source):
        pltpu.make_async_remote_copy(
            src_ref=place(slot, source),
            dst_ref=place(slot, source),
            send_sem=kv_send.at[slot, source],
            recv_sem=kv_recv.at[slot, source],
            device_id={"patch": source},
            device_id_type=MESH,
        ).wait_recv()

    def receive_kv(step, unused):
        source = lax.rem(me + step, size)
        kv_wait(0, source)

        @pl.when(my_last != my_first)
        def _():
            kv_wait(1, source)

        return unused

    lax.fori_loop(1, size, receive_kv, 0)

    def run_task(index, unused):
        task = me * pairs + index
        pair = lax.div(task, size)
        owner = lax.rem(task, size)
        slot = pair - my_first
        pltpu.make_async_copy(q_in.at[index], q_in.at[index], q_recv.at[index]).wait()
        queries = heads_of(q_in[index])

        def partial(step):
            at = pl.ds(pl.multiple_of(lax.rem(owner + step, size) * block, block), block)
            return kvs[slot, 0, at, :], jnp.concatenate([kvs[slot, 1, at, :], ones], axis=1)

        keys, values = partial(1)
        for head in range(2):
            scores = scores_of(queries[head], keys)
            height = jnp.max(scores, axis=1, keepdims=True)
            weights = jnp.exp2((scores - height) * EXP_SCALE).astype(BF16)
            acc[head] = dot(weights, values)
            top[head] = jnp.broadcast_to(height, (block, LANES))

        def more(step, unused):
            keys, values = partial(step)
            for head in range(2):
                scores = scores_of(queries[head], keys)
                before = top[head]
                height = jnp.maximum(before, jnp.max(scores, axis=1, keepdims=True))
                factor = jnp.exp2((before - height) * EXP_SCALE)
                weights = jnp.exp2((scores - height[:, :1]) * EXP_SCALE).astype(BF16)
                summed = dot(weights, values)
                acc[head, :, :LANES] = acc[head, :, :LANES] * factor + summed[:, :LANES]
                acc[head, :, LANES:] = acc[head, :, LANES:] * factor + summed[:, LANES:]
                top[head] = height
            return unused

        lax.fori_loop(2, size, more, 0)
        value, lse = finish([(acc[0], top[0]), (acc[1], top[1])])
        res[index] = value.astype(BF16)
        turned = jnp.transpose(lse)
        res_lse[index, 0:8] = turned[0:8]
        res_lse[index, 8:16] = turned[HEAD_DIM : HEAD_DIM + 8]

        @pl.when(owner != me)
        def _():
            for copy in result_copies(index, pair, owner):
                copy.start()

        @pl.when(owner == me)
        def _():
            pltpu.make_async_copy(res.at[index], res_in.at[pair], res_recv.at[pair]).start()
            pltpu.make_async_copy(res_lse.at[index], lse_in.at[pair], lse_recv.at[pair]).start()

        return unused

    def result_copies(index, pair, owner):
        return [
            pltpu.make_async_remote_copy(
                src_ref=source.at[index],
                dst_ref=into.at[pair],
                send_sem=sent.at[index],
                recv_sem=received.at[pair],
                device_id={"patch": owner},
                device_id_type=MESH,
            )
            for source, into, sent, received in (
                (res, res_in, res_send, res_recv),
                (res_lse, lse_in, lse_send, lse_recv),
            )
        ]

    lax.fori_loop(0, pairs, run_task, 0)

    output = mixed[...]
    for pair in range(pairs):
        pltpu.make_async_copy(res_in.at[pair], res_in.at[pair], res_recv.at[pair]).wait()
        pltpu.make_async_copy(lse_in.at[pair], lse_in.at[pair], lse_recv.at[pair]).wait()
    merged = []
    for pair in range(pairs):
        rows = lax.broadcasted_iota(jnp.int32, (LANES, block), 0) < HEAD_DIM
        lse = jnp.transpose(jnp.where(rows, lse_in[pair, 0:1], lse_in[pair, 8:9]))
        mine = own_lse[pair]
        best = jnp.maximum(lse, mine)
        there = jnp.exp(lse - best)
        here = jnp.exp(mine - best)
        value = (there * res_in[pair].astype(F32) + here * own_val[pair]) / (there + here)
        merged.append(value.astype(BF16))
    out_ref[...] = (output + dot(jnp.concatenate(merged, axis=1), projw[3])).astype(BF16)

    def sent_kv(step, unused):
        target = lax.rem(me + step, size)
        kv_copy(0, first_pair(target), target, me).wait_send()

        @pl.when(last_pair(target) != first_pair(target))
        def _():
            kv_copy(1, last_pair(target), target, me).wait_send()

        return unused

    lax.fori_loop(1, size, sent_kv, 0)
    for pair in range(pairs):
        target, slot = task_of(pair)

        @pl.when(target != me)
        def _():
            q_remote(pair, target, slot).wait_send()

        task = me * pairs + pair
        owner = lax.rem(task, size)

        @pl.when(owner != me)
        def _():
            for copy in result_copies(pair, lax.div(task, size), owner):
                copy.wait_send()


def on_device(
    features,
    stale_kv,
    timestep,
    time_w,
    gain_one,
    conv_w,
    shortcut_w,
    gain_two,
    query_w,
    key_w,
    value_w,
    out_w,
):
    rows, cols, width_in = features.shape
    width = shortcut_w.shape[1]
    block = rows * cols
    size = lax.axis_size("patch")
    pairs = width // LANES
    half = FREQ // 2
    freqs = jnp.exp(-math.log(10000.0) * jnp.arange(half, dtype=F32) / half)
    angles = timestep.astype(F32)[0] * freqs
    embed = jnp.concatenate([jnp.cos(angles), jnp.sin(angles)]).astype(BF16)
    embed = jnp.broadcast_to(embed[None, :], (16, FREQ))
    anywhere = pl.BlockSpec(memory_space=pl.ANY)
    vmem = pl.BlockSpec(memory_space=pltpu.VMEM)
    dma = pltpu.SemaphoreType.DMA
    flops = 2 * block * width * (10 * width_in + 4 * width + 4 * size * block)
    output = pl.pallas_call(
        functools.partial(fused_kernel, size),
        out_shape=jax.ShapeDtypeStruct((block, width), BF16),
        in_specs=[anywhere, anywhere, vmem, vmem, vmem, anywhere, anywhere, vmem]
        + [anywhere] * 4,
        out_specs=vmem,
        scratch_shapes=[
            pltpu.VMEM((block, width_in), BF16),
            pltpu.VMEM((3, 3, width_in, width), BF16),
            pltpu.VMEM((width_in, width), BF16),
            pltpu.VMEM((4, width, width), BF16),
            pltpu.VMEM((block + 2 * cols, width_in), BF16),
            pltpu.VMEM((3, block, width), F32),
            pltpu.VMEM((block, width), F32),
            pltpu.VMEM((2, 2, size * block, LANES), BF16),
            pltpu.VMEM((8, width_in), F32),
            pltpu.VMEM((size, 8, width_in), F32),
            pltpu.VMEM((8, width), F32),
            pltpu.VMEM((size, 8, width), F32),
            pltpu.VMEM((3, pairs, block, LANES), BF16),
            pltpu.VMEM((pairs, block, LANES), BF16),
            pltpu.VMEM((pairs, block, LANES), F32),
            pltpu.VMEM((pairs, block, LANES), F32),
            pltpu.VMEM((2, block, 2 * LANES), F32),
            pltpu.VMEM((2, block, LANES), F32),
            pltpu.VMEM((pairs, block, LANES), BF16),
            pltpu.VMEM((pairs, 16, block), F32),
            pltpu.VMEM((pairs, block, LANES), BF16),
            pltpu.VMEM((pairs, 16, block), F32),
            dma((6,)),
            dma((3, 3)),
            dma((2, size)),
            dma((2, size)),
            dma((2,)),
            dma((2, size)),
            dma((2, size)),
            dma((2,)),
            dma((2,)),
            dma((pairs,)),
            dma((pairs,)),
            dma((pairs,)),
            dma((pairs,)),
            dma((pairs,)),
            dma((pairs,)),
        ],
        compiler_params=pltpu.CompilerParams(
            collective_id=0, has_side_effects=True, vmem_limit_bytes=58 * 1024 * 1024
        ),
        cost_estimate=pl.CostEstimate(
            flops=flops, bytes_accessed=24_000_000, transcendentals=block * size * block * 10
        ),
    )(
        stale_kv,
        features.reshape(block, width_in),
        embed,
        time_w,
        gain_one[None, :],
        conv_w,
        shortcut_w,
        gain_two[None, :],
        query_w,
        key_w,
        value_w,
        out_w,
    )
    return output.reshape(rows, cols, width)


def solution(mesh):
    return jax.shard_map(
        on_device,
        mesh=mesh,
        in_specs=(
            P("patch", "batch", None),
            P("batch", "patch", None),
            P("batch"),
            P(),
            P(),
            P(),
            P(),
            P(),
            P(),
            P(),
            P(),
            P(),
        ),
        out_specs=P("patch", "batch", None),
        check_vma=False,
    )
```

```python
import functools
import math

import jax
import jax.numpy as jnp
from jax import lax
from jax.experimental import pallas as pl
from jax.experimental.pallas import tpu as pltpu
from jax.sharding import PartitionSpec as P

HEAD_DIM = 64
GROUPS = 32
FREQ = 320
LANES = 128
F32 = jnp.float32
BF16 = jnp.bfloat16
EXP_SCALE = 0.125 * math.log2(math.e)
LN2 = math.log(2.0)
MESH = pl.DeviceIdType.MESH


def dot(a, b):
    return jnp.dot(a, b, preferred_element_type=F32)


def split_dot(a, b):
    high = a.astype(BF16)
    rest = a - high.astype(F32)
    mid = rest.astype(BF16)
    low = rest - mid.astype(F32)
    stacked = jnp.concatenate([high.astype(F32), mid.astype(F32), low, jnp.zeros_like(a)], axis=0)
    out = dot(stacked.astype(BF16), b)
    return out[0:8] + out[8:16] + out[16:24]


def swap(x):
    return pltpu.roll(x.astype(F32), HEAD_DIM, 1)


def fold(x, side):
    rows = x.shape[0] // 2
    upper, lower = x[:rows].astype(F32), x[rows:].astype(F32)
    mask = half_mask(rows)
    if side == 0:
        return jnp.where(mask, upper, swap(lower)).astype(BF16)
    return jnp.where(mask, swap(upper), lower).astype(BF16)


def members(shape, chan_dim, size):
    chan = lax.broadcasted_iota(jnp.int32, shape, chan_dim)
    group = lax.broadcasted_iota(jnp.int32, shape, 1 - chan_dim) * size
    return jnp.where((chan >= group) & (chan < group + size), 1.0, 0.0).astype(BF16)


def two_rows(first, second):
    row = lax.broadcasted_iota(jnp.int32, (8, first.shape[1]), 0)
    return jnp.where(row == 0, first, jnp.where(row == 1, second, 0.0))


def group_sums(total):
    width = total.shape[1]
    return split_dot(total, members((width, LANES), 0, width // GROUPS))


def group_stats(grouped, count, width, eps):
    center = grouped[0:1] / count
    spread = jnp.maximum(grouped[1:2] / count - center * center, 0.0)
    size = width // GROUPS
    wide = split_dot(two_rows(center, lax.rsqrt(spread + eps)), members((LANES, width), 1, size))
    return wide[0:1], wide[1:2]


def half_mask(rows):
    return lax.broadcasted_iota(jnp.int32, (rows, LANES), 1) < HEAD_DIM


def scores_of(query, keys):
    return lax.dot_general(query, keys, (((1,), (1,)), ((), ())), preferred_element_type=F32)


def fused_kernel(
    size,
    kv_ref,
    feat_ref,
    embed_ref,
    time_ref,
    gain_one_ref,
    conv_ref,
    short_ref,
    gain_two_ref,
    qw_ref,
    kw_ref,
    vw_ref,
    ow_ref,
    out_ref,
    feat,
    convw,
    shortw,
    projw,
    act,
    parts,
    mixed,
    kvs,
    stale,
    packed,
    stat_out1,
    stat_in1,
    stat_out2,
    stat_in2,
    fresh,
    q_out,
    q_in,
    own_val,
    own_lse,
    acc,
    top,
    res,
    res_lse,
    res_in,
    lse_in,
    load_sem,
    conv_sem,
    kv_send,
    kv_recv,
    stat_send,
    stat_recv,
    halo_send,
    halo_recv,
    q_send,
    q_recv,
    res_send,
    res_recv,
    lse_send,
    lse_recv,
):
    me = lax.axis_index("patch")
    block, width = out_ref.shape
    width_in = feat.shape[1]
    pairs = width // LANES
    heads = width // HEAD_DIM
    slots = kvs.shape[0]
    cols = (act.shape[0] - block) // 2
    inside = pl.ds(cols, block)

    loads = [
        pltpu.make_async_copy(feat_ref, feat.at[pl.ds(cols, block), :], load_sem.at[0]),
        pltpu.make_async_copy(short_ref, shortw, load_sem.at[1]),
        pltpu.make_async_copy(qw_ref, projw.at[0], load_sem.at[2]),
        pltpu.make_async_copy(kw_ref, projw.at[1], load_sem.at[3]),
        pltpu.make_async_copy(vw_ref, projw.at[2], load_sem.at[4]),
        pltpu.make_async_copy(ow_ref, projw.at[3], load_sem.at[5]),
    ]
    conv_loads = [
        [
            pltpu.make_async_copy(conv_ref.at[dy, dx], convw.at[dy, dx], conv_sem.at[dy, dx])
            for dx in range(3)
        ]
        for dy in range(3)
    ]
    stale_load = pltpu.make_async_copy(kv_ref, stale, load_sem.at[6])
    stale_load.start()
    loads[0].start()
    loads[1].start()
    for dy in (1, 0, 2):
        for dx in range(3):
            conv_loads[dy][dx].start()
    for load in loads[2:]:
        load.start()

    barrier = pltpu.get_barrier_semaphore()

    def greet(step, unused):
        pl.semaphore_signal(
            barrier, inc=1, device_id={"patch": lax.rem(me + step, size)}, device_id_type=MESH
        )
        return unused

    lax.fori_loop(1, size, greet, 0)

    def first_head(device):
        return lax.div(device * heads, size)

    def last_head(device):
        return lax.div(device * heads + heads - 1, size)

    def place(slot, owner):
        return kvs.at[slot, pl.ds(pl.multiple_of(owner * block, block), block), :]

    def kv_copy(slot, target):
        return pltpu.make_async_remote_copy(
            src_ref=packed.at[first_head(target) + slot],
            dst_ref=place(slot, me),
            send_sem=kv_send.at[slot, target],
            recv_sem=kv_recv.at[slot, me],
            device_id={"patch": target},
            device_id_type=MESH,
        )

    my_first = first_head(me)
    my_last = last_head(me)

    def pack_kv(step, unused):
        lanes = pl.ds(pl.multiple_of(step * LANES, LANES), LANES)
        keys = stale[0, :, lanes].astype(F32)
        values = stale[1, :, lanes].astype(F32)
        mask = half_mask(block)
        packed[2 * step] = jnp.where(mask, keys, swap(values)).astype(BF16)
        packed[2 * step + 1] = jnp.where(mask, swap(keys), values).astype(BF16)
        return unused

    stale_load.wait()
    lax.fori_loop(0, pairs, pack_kv, 0)
    for slot in range(slots):

        @pl.when(my_first + slot <= my_last)
        def _():
            kvs[slot, pl.ds(pl.multiple_of(me * block, block), block), :] = packed[my_first + slot]


    loads[0].wait()

    @pl.when(me == 0)
    def _():
        feat[0:cols, :] = jnp.zeros((cols, width_in), BF16)

    @pl.when(me == size - 1)
    def _():
        feat[block + cols : block + 2 * cols, :] = jnp.zeros((cols, width_in), BF16)

    def sum_rows(step, carry):
        first, second = carry
        x = feat[pl.ds(pl.multiple_of(cols + step * 16, 16), 16), :].astype(F32)
        low, high = x[:8], x[8:]
        return first + (low + high), second + (low * low + high * high)

    zero = jnp.zeros((8, width_in), F32)
    first, second = lax.fori_loop(0, block // 16, sum_rows, (zero, zero))
    sums = two_rows(
        jnp.sum(first, axis=0, keepdims=True), jnp.sum(second, axis=0, keepdims=True)
    )
    stat_out1[...] = group_sums(sums)
    pl.semaphore_wait(barrier, size - 1)

    def stat_copy(which, out, into, target, index):
        return pltpu.make_async_remote_copy(
            src_ref=out,
            dst_ref=into.at[me],
            send_sem=stat_send.at[which, target],
            recv_sem=stat_recv.at[which, index],
            device_id={"patch": target},
            device_id_type=MESH,
        )

    def stats_start(which, out, into):
        def send(step, unused):
            target = lax.rem(me + step, size)
            stat_copy(which, out, into, target, me).start()
            return unused

        lax.fori_loop(1, size, send, 0)

    def stats_finish(which, out, into):
        def receive(step, total):
            source = lax.rem(me + step, size)
            pltpu.make_async_remote_copy(
                src_ref=out,
                dst_ref=into.at[source],
                send_sem=stat_send.at[which, source],
                recv_sem=stat_recv.at[which, source],
                device_id={"patch": source},
                device_id_type=MESH,
            ).wait()
            return total + into[source]

        return lax.fori_loop(1, size, receive, out[...])

    stats_start(0, stat_out1, stat_in1)

    top_row = feat.at[pl.ds(cols, cols), :]
    bottom_row = feat.at[pl.ds(block, cols), :]
    above = feat.at[pl.ds(0, cols), :]
    below = feat.at[pl.ds(block + cols, cols), :]
    up = pltpu.make_async_remote_copy(
        src_ref=top_row,
        dst_ref=below,
        send_sem=halo_send.at[0],
        recv_sem=halo_recv.at[0],
        device_id={"patch": lax.rem(me + size - 1, size)},
        device_id_type=MESH,
    )
    down = pltpu.make_async_remote_copy(
        src_ref=bottom_row,
        dst_ref=above,
        send_sem=halo_send.at[1],
        recv_sem=halo_recv.at[1],
        device_id={"patch": lax.rem(me + 1, size)},
        device_id_type=MESH,
    )

    @pl.when(me > 0)
    def _():
        up.start()

    @pl.when(me < size - 1)
    def _():
        down.start()

    def send_kv(step, unused):
        target = lax.rem(me + step, size)
        kv_copy(0, target).start()
        for slot in range(1, slots):

            @pl.when(first_head(target) + slot <= last_head(target))
            def _():
                kv_copy(slot, target).start()

        return unused

    lax.fori_loop(1, size, send_kv, 0)

    loads[1].wait()
    mixed[...] = dot(feat[inside, :], shortw[...]) + dot(embed_ref[...], time_ref[...])[0:1]

    total = stats_finish(0, stat_out1, stat_in1)
    count = float(size * block * (width_in // GROUPS))
    center, inverse = group_stats(total, count, width_in, 1e-05)
    scale = inverse * gain_one_ref[...].reshape(1, width_in)

    @pl.when(me > 0)
    def _():
        up.wait_send()
        down.wait_recv()

    @pl.when(me < size - 1)
    def _():
        down.wait_send()
        up.wait_recv()

    def activate(step, unused):
        x = feat[pl.ds(pl.multiple_of(step * 16, 16), 16), :].astype(F32)
        y = (x - center) * scale
        half = 0.5 * y
        z = half + half * jnp.tanh(half)
        act[pl.ds(pl.multiple_of(step * 16, 16), 16), :] = z.astype(BF16)
        return unused

    lax.fori_loop(0, act.shape[0] // 16, activate, 0)

    @pl.when(me == 0)
    def _():
        act[0:cols, :] = jnp.zeros((cols, width_in), BF16)

    @pl.when(me == size - 1)
    def _():
        act[block + cols : block + 2 * cols, :] = jnp.zeros((cols, width_in), BF16)

    for dx in range(3):
        conv_loads[1][dx].wait()

    def middle(dx, unused):
        parts[dx] = dot(act[pl.ds(cols, block), :], convw[1, dx])
        return unused

    lax.fori_loop(0, 3, middle, 0)

    for dy in (0, 2):
        for dx in range(3):
            conv_loads[dy][dx].wait()

    def outer(dx, unused):
        parts[dx] = (
            parts[dx]
            + dot(act[pl.ds(0, block), :], convw[0, dx])
            + dot(act[pl.ds(2 * cols, block), :], convw[2, dx])
        )
        return unused

    lax.fori_loop(0, 3, outer, 0)

    col = lax.rem(lax.broadcasted_iota(jnp.int32, (block, LANES), 0), cols)
    sums = []
    for pair in range(pairs):
        lanes = pl.ds(pair * LANES, LANES)
        left = jnp.where(col == 0, 0.0, pltpu.roll(parts[0, :, lanes], 1, 0))
        right = jnp.where(col == cols - 1, 0.0, pltpu.roll(parts[2, :, lanes], block - 1, 0))
        value = mixed[:, lanes] + (left + parts[1, :, lanes] + right)
        mixed[:, lanes] = value
        sums.append(
            two_rows(
                jnp.sum(value, axis=0, keepdims=True),
                jnp.sum(value * value, axis=0, keepdims=True),
            )
        )
    stat_out2[...] = group_sums(jnp.concatenate(sums, axis=1))
    stats_start(1, stat_out2, stat_in2)
    for load in loads[2:]:
        load.wait()
    total = stats_finish(1, stat_out2, stat_in2)
    count = float(size * block * (width // GROUPS))
    center, inverse = group_stats(total, count, width, 1e-06)
    normed = ((mixed[...] - center) * (inverse * gain_two_ref[...].reshape(1, width))).astype(BF16)

    def task_of(head):
        task = head * size + me
        return lax.div(task, heads), lax.rem(task, heads)

    def q_remote(head, target, slot):
        return pltpu.make_async_remote_copy(
            src_ref=q_out.at[head],
            dst_ref=q_in.at[slot],
            send_sem=q_send.at[head],
            recv_sem=q_recv.at[slot],
            device_id={"patch": target},
            device_id_type=MESH,
        )

    queries = dot(normed, projw[0]).astype(BF16)
    for pair in range(pairs):
        both = queries[:, pair * LANES : (pair + 1) * LANES]
        fresh[0, pair] = both
        q_out[2 * pair] = fold(both, 0)
        q_out[2 * pair + 1] = fold(both, 1)

    def send_queries(head, unused):
        target, slot = task_of(head)

        @pl.when(target != me)
        def _():
            q_remote(head, target, slot).start()

        @pl.when(target == me)
        def _():
            pltpu.make_async_copy(q_out.at[head], q_in.at[slot], q_recv.at[slot]).start()

        return unused

    lax.fori_loop(0, heads, send_queries, 0)

    for kind in (1, 2):
        value = dot(normed, projw[kind]).astype(BF16)
        for pair in range(pairs):
            fresh[kind, pair] = value[:, pair * LANES : (pair + 1) * LANES]

    left_half = half_mask(block)
    ones = jnp.ones((block, LANES), BF16)

    def heads_of(query):
        none = jnp.zeros_like(query)
        return jnp.where(left_half, query, none), jnp.where(left_half, none, query)

    def finish(pieces):
        values, lses = [], []
        for summed, height in pieces:
            weight = summed[:, LANES:]
            values.append(summed[:, :LANES] / weight)
            lses.append(height * 0.125 + jnp.log(weight))
        return jnp.where(left_half, *values), jnp.where(left_half, *lses)

    def own_attention(pair, unused):
        keys = fresh[1, pair]
        values = jnp.concatenate([fresh[2, pair], ones], axis=1)
        pieces = []
        for query in heads_of(fresh[0, pair]):
            scores = scores_of(query, keys)
            height = jnp.max(scores, axis=1, keepdims=True)
            weights = jnp.exp2((scores - height) * EXP_SCALE).astype(BF16)
            pieces.append((dot(weights, values), jnp.broadcast_to(height, (block, LANES))))
        own_val[pair], own_lse[pair] = finish(pieces)
        return unused

    lax.fori_loop(0, pairs, own_attention, 0)

    def kv_wait(slot, source):
        pltpu.make_async_remote_copy(
            src_ref=place(slot, source),
            dst_ref=place(slot, source),
            send_sem=kv_send.at[slot, source],
            recv_sem=kv_recv.at[slot, source],
            device_id={"patch": source},
            device_id_type=MESH,
        ).wait_recv()

    def receive_kv(step, unused):
        source = lax.rem(me + step, size)
        kv_wait(0, source)
        for slot in range(1, slots):

            @pl.when(my_first + slot <= my_last)
            def _():
                kv_wait(slot, source)

        return unused

    lax.fori_loop(1, size, receive_kv, 0)

    def place_of(index):
        task = me * heads + index
        return lax.div(task, size), lax.rem(task, size)

    def unfold(x):
        mask = half_mask(block // 2)
        upper = jnp.where(mask, x.astype(F32), 0.0)
        lower = jnp.where(mask, swap(x), 0.0)
        return jnp.concatenate([upper, lower], axis=0).astype(BF16)

    def run_tasks(couple, unused):
        tasks = []
        for which in range(2):
            index = 2 * couple + which
            head, owner = place_of(index)
            pltpu.make_async_copy(q_in.at[index], q_in.at[index], q_recv.at[index]).wait()
            tasks.append((head - my_first, owner, unfold(q_in[index])))

        def partial(slot, owner, step):
            rows = pl.ds(pl.multiple_of(lax.rem(owner + step, size) * block, block), block)
            both = kvs[slot, rows, :]
            return both, jnp.where(left_half, ones, both)

        for which, (slot, owner, query) in enumerate(tasks):
            keys, values = partial(slot, owner, 1)
            scores = scores_of(query, keys)
            height = jnp.max(scores, axis=1, keepdims=True)
            weights = jnp.exp2((scores - height) * EXP_SCALE).astype(BF16)
            acc[which] = dot(weights, values)
            top[which] = jnp.broadcast_to(height, (block, LANES))

        def more(step, unused):
            for which, (slot, owner, query) in enumerate(tasks):
                keys, values = partial(slot, owner, step)
                scores = scores_of(query, keys)
                before = top[which]
                height = jnp.maximum(before, jnp.max(scores, axis=1, keepdims=True))
                factor = jnp.exp2((before - height) * EXP_SCALE)
                weights = jnp.exp2((scores - height[:, :1]) * EXP_SCALE).astype(BF16)
                acc[which] = acc[which] * factor + dot(weights, values)
                top[which] = height
            return unused

        lax.fori_loop(2, size, more, 0)
        lses = []
        for which in range(2):
            index = 2 * couple + which
            summed = acc[which]
            total = swap(summed)
            res[index] = fold(summed / total, 1)
            lses.append(top[which] * 0.125 + jnp.log(total))
        turned = jnp.transpose(jnp.where(left_half, swap(lses[0]), lses[1]))
        res_lse[2 * couple] = turned[0:8]
        res_lse[2 * couple + 1] = turned[HEAD_DIM : HEAD_DIM + 8]
        for which in range(2):
            index = 2 * couple + which
            head, owner = place_of(index)

            @pl.when(owner != me)
            def _():
                for copy in result_copies(index, head, owner):
                    copy.start()

            @pl.when(owner == me)
            def _():
                pltpu.make_async_copy(res.at[index], res_in.at[head], res_recv.at[head]).start()
                pltpu.make_async_copy(
                    res_lse.at[index], lse_in.at[head], lse_recv.at[head]
                ).start()

        return unused

    def result_copies(index, head, owner):
        return [
            pltpu.make_async_remote_copy(
                src_ref=source.at[index],
                dst_ref=into.at[head],
                send_sem=sent.at[index],
                recv_sem=received.at[head],
                device_id={"patch": owner},
                device_id_type=MESH,
            )
            for source, into, sent, received in (
                (res, res_in, res_send, res_recv),
                (res_lse, lse_in, lse_send, lse_recv),
            )
        ]

    lax.fori_loop(0, pairs, run_tasks, 0)

    output = mixed[...]
    for pair in range(heads):
        pltpu.make_async_copy(res_in.at[pair], res_in.at[pair], res_recv.at[pair]).wait()
        pltpu.make_async_copy(lse_in.at[pair], lse_in.at[pair], lse_recv.at[pair]).wait()
    merged = []
    for pair in range(pairs):
        rows = lax.broadcasted_iota(jnp.int32, (LANES, block), 0) < HEAD_DIM
        lse = jnp.transpose(jnp.where(rows, lse_in[2 * pair, 0:1], lse_in[2 * pair + 1, 0:1]))
        mine = own_lse[pair]
        best = jnp.maximum(lse, mine)
        there = jnp.exp(lse - best)
        here = jnp.exp(mine - best)
        first, second = res_in[2 * pair].astype(F32), res_in[2 * pair + 1].astype(F32)
        mask = half_mask(block // 2)
        upper = jnp.where(mask, first, swap(second))
        lower = jnp.where(mask, swap(first), second)
        value = (there * jnp.concatenate([upper, lower], axis=0) + here * own_val[pair]) / (there + here)
        merged.append(value.astype(BF16))
    out_ref[...] = (output + dot(jnp.concatenate(merged, axis=1), projw[3])).astype(BF16)

    def sent_kv(step, unused):
        target = lax.rem(me + step, size)
        kv_copy(0, target).wait_send()
        for slot in range(1, slots):

            @pl.when(first_head(target) + slot <= last_head(target))
            def _():
                kv_copy(slot, target).wait_send()

        return unused

    lax.fori_loop(1, size, sent_kv, 0)

    def sent_rest(index, unused):
        target, slot = task_of(index)

        @pl.when(target != me)
        def _():
            q_remote(index, target, slot).wait_send()

        head, owner = place_of(index)

        @pl.when(owner != me)
        def _():
            for copy in result_copies(index, head, owner):
                copy.wait_send()

        return unused

    lax.fori_loop(0, heads, sent_rest, 0)


def slots_for(heads, size):
    return max(
        (device * heads + heads - 1) // size - device * heads // size + 1
        for device in range(size)
    )


def on_device(
    features,
    stale_kv,
    timestep,
    time_w,
    gain_one,
    conv_w,
    shortcut_w,
    gain_two,
    query_w,
    key_w,
    value_w,
    out_w,
):
    rows, cols, width_in = features.shape
    width = shortcut_w.shape[1]
    block = rows * cols
    size = lax.axis_size("patch")
    pairs = width // LANES
    heads = width // HEAD_DIM
    half = FREQ // 2
    freqs = jnp.exp(-math.log(10000.0) * jnp.arange(half, dtype=F32) / half)
    angles = timestep.astype(F32)[0] * freqs
    embed = jnp.concatenate([jnp.cos(angles), jnp.sin(angles)]).astype(BF16)
    embed = jnp.broadcast_to(embed[None, :], (16, FREQ))
    anywhere = pl.BlockSpec(memory_space=pl.ANY)
    vmem = pl.BlockSpec(memory_space=pltpu.VMEM)
    dma = pltpu.SemaphoreType.DMA
    flops = 2 * block * width * (10 * width_in + 4 * width + 4 * size * block)
    output = pl.pallas_call(
        functools.partial(fused_kernel, size),
        out_shape=jax.ShapeDtypeStruct((block, width), BF16),
        in_specs=[anywhere, anywhere, vmem, vmem, vmem, anywhere, anywhere, vmem]
        + [anywhere] * 4,
        out_specs=vmem,
        scratch_shapes=[
            pltpu.VMEM((block + 2 * cols, width_in), BF16),
            pltpu.VMEM((3, 3, width_in, width), BF16),
            pltpu.VMEM((width_in, width), BF16),
            pltpu.VMEM((4, width, width), BF16),
            pltpu.VMEM((block + 2 * cols, width_in), BF16),
            pltpu.VMEM((3, block, width), F32),
            pltpu.VMEM((block, width), F32),
            pltpu.VMEM((slots_for(heads, size), size * block, LANES), BF16),
            pltpu.VMEM((2, block, width), BF16),
            pltpu.VMEM((heads, block, LANES), BF16),
            pltpu.VMEM((8, LANES), F32),
            pltpu.VMEM((size, 8, LANES), F32),
            pltpu.VMEM((8, LANES), F32),
            pltpu.VMEM((size, 8, LANES), F32),
            pltpu.VMEM((3, pairs, block, LANES), BF16),
            pltpu.VMEM((heads, block // 2, LANES), BF16),
            pltpu.VMEM((heads, block // 2, LANES), BF16),
            pltpu.VMEM((pairs, block, LANES), F32),
            pltpu.VMEM((pairs, block, LANES), F32),
            pltpu.VMEM((2, block, LANES), F32),
            pltpu.VMEM((2, block, LANES), F32),
            pltpu.VMEM((heads, block // 2, LANES), BF16),
            pltpu.VMEM((heads, 8, block), F32),
            pltpu.VMEM((heads, block // 2, LANES), BF16),
            pltpu.VMEM((heads, 8, block), F32),
            dma((7,)),
            dma((3, 3)),
            dma((slots_for(heads, size), size)),
            dma((slots_for(heads, size), size)),
            dma((2, size)),
            dma((2, size)),
            dma((2,)),
            dma((2,)),
            dma((heads,)),
            dma((heads,)),
            dma((heads,)),
            dma((heads,)),
            dma((heads,)),
            dma((heads,)),
        ],
        compiler_params=pltpu.CompilerParams(
            collective_id=0, has_side_effects=True, vmem_limit_bytes=58 * 1024 * 1024
        ),
        cost_estimate=pl.CostEstimate(
            flops=flops, bytes_accessed=24_000_000, transcendentals=block * size * block * 10
        ),
    )(
        stale_kv,
        features.reshape(block, width_in),
        embed,
        time_w,
        gain_one,
        conv_w,
        shortcut_w,
        gain_two,
        query_w,
        key_w,
        value_w,
        out_w,
    )
    return output.reshape(rows, cols, width)


def solution(mesh):
    return jax.shard_map(
        on_device,
        mesh=mesh,
        in_specs=(
            P("patch", "batch", None),
            P("batch", "patch", None),
            P("batch"),
            P(),
            P(),
            P(),
            P(),
            P(),
            P(),
            P(),
            P(),
            P(),
        ),
        out_specs=P("patch", "batch", None),
        check_vma=False,
    )
```

```python
import functools
import math

import jax
import jax.numpy as jnp
from jax import lax
from jax.experimental import pallas as pl
from jax.experimental.pallas import tpu as pltpu
from jax.sharding import PartitionSpec as P

HEAD_DIM = 64
GROUPS = 32
FREQ = 320
LANES = 128
F32 = jnp.float32
BF16 = jnp.bfloat16
EXP_SCALE = 0.125 * math.log2(math.e)
LN2 = math.log(2.0)
MESH = pl.DeviceIdType.MESH


def dot(a, b):
    return jnp.dot(a, b, preferred_element_type=F32)


def split_dot(a, b):
    high = a.astype(BF16)
    rest = a - high.astype(F32)
    mid = rest.astype(BF16)
    low = rest - mid.astype(F32)
    stacked = jnp.concatenate([high.astype(F32), mid.astype(F32), low, jnp.zeros_like(a)], axis=0)
    out = dot(stacked.astype(BF16), b)
    return out[0:8] + out[8:16] + out[16:24]


def swap(x):
    return pltpu.roll(x.astype(F32), HEAD_DIM, 1)


def fold(x, side):
    rows = x.shape[0] // 2
    upper, lower = x[:rows].astype(F32), x[rows:].astype(F32)
    mask = half_mask(rows)
    if side == 0:
        return jnp.where(mask, upper, swap(lower)).astype(BF16)
    return jnp.where(mask, swap(upper), lower).astype(BF16)


def members(shape, chan_dim, size):
    chan = lax.broadcasted_iota(jnp.int32, shape, chan_dim)
    group = lax.broadcasted_iota(jnp.int32, shape, 1 - chan_dim) * size
    return jnp.where((chan >= group) & (chan < group + size), 1.0, 0.0).astype(BF16)


def two_rows(first, second):
    row = lax.broadcasted_iota(jnp.int32, (8, first.shape[1]), 0)
    return jnp.where(row == 0, first, jnp.where(row == 1, second, 0.0))


def group_sums(total):
    width = total.shape[1]
    return split_dot(total, members((width, LANES), 0, width // GROUPS))


def group_stats(grouped, count, width, eps):
    center = grouped[0:1] / count
    spread = jnp.maximum(grouped[1:2] / count - center * center, 0.0)
    size = width // GROUPS
    wide = split_dot(two_rows(center, lax.rsqrt(spread + eps)), members((LANES, width), 1, size))
    return wide[0:1], wide[1:2]


def half_mask(rows):
    return lax.broadcasted_iota(jnp.int32, (rows, LANES), 1) < HEAD_DIM


def scores_of(query, keys):
    return lax.dot_general(query, keys, (((1,), (1,)), ((), ())), preferred_element_type=F32)


def fused_kernel(
    size,
    kv_ref,
    feat_ref,
    embed_ref,
    time_ref,
    gain_one_ref,
    conv_ref,
    short_ref,
    gain_two_ref,
    qw_ref,
    kw_ref,
    vw_ref,
    ow_ref,
    out_ref,
    feat,
    convw,
    shortw,
    projw,
    act,
    parts,
    mixed,
    kvs,
    stale,
    packed,
    stat_out1,
    stat_in1,
    stat_out2,
    stat_in2,
    fresh,
    q_out,
    q_in,
    own_val,
    own_lse,
    acc,
    top,
    res,
    res_lse,
    res_in,
    lse_in,
    load_sem,
    conv_sem,
    kv_send,
    kv_recv,
    stat_send,
    stat_recv,
    halo_send,
    halo_recv,
    q_send,
    q_recv,
    res_send,
    res_recv,
    lse_send,
    lse_recv,
):
    me = lax.axis_index("patch")
    block, width = out_ref.shape
    width_in = feat.shape[1]
    pairs = width // LANES
    heads = width // HEAD_DIM
    slots = kvs.shape[0]
    cols = (act.shape[0] - block) // 2
    inside = pl.ds(cols, block)

    loads = [
        pltpu.make_async_copy(feat_ref, feat.at[pl.ds(cols, block), :], load_sem.at[0]),
        pltpu.make_async_copy(short_ref, shortw, load_sem.at[1]),
        pltpu.make_async_copy(qw_ref, projw.at[0], load_sem.at[2]),
        pltpu.make_async_copy(kw_ref, projw.at[1], load_sem.at[3]),
        pltpu.make_async_copy(vw_ref, projw.at[2], load_sem.at[4]),
        pltpu.make_async_copy(ow_ref, projw.at[3], load_sem.at[5]),
    ]
    conv_loads = [
        [
            pltpu.make_async_copy(conv_ref.at[dy, dx], convw.at[dy, dx], conv_sem.at[dy, dx])
            for dx in range(3)
        ]
        for dy in range(3)
    ]
    stale_load = pltpu.make_async_copy(kv_ref, stale, load_sem.at[6])
    stale_load.start()
    loads[0].start()
    loads[1].start()
    for dy in (1, 0, 2):
        for dx in range(3):
            conv_loads[dy][dx].start()
    for load in loads[2:]:
        load.start()

    barrier = pltpu.get_barrier_semaphore()

    def greet(step, unused):
        pl.semaphore_signal(
            barrier, inc=1, device_id={"patch": lax.rem(me + step, size)}, device_id_type=MESH
        )
        return unused

    lax.fori_loop(1, size, greet, 0)

    def first_head(device):
        return lax.div(device * heads, size)

    def last_head(device):
        return lax.div(device * heads + heads - 1, size)

    def place(slot, owner):
        return kvs.at[slot, pl.ds(pl.multiple_of(owner * block, block), block), :]

    def kv_copy(slot, target):
        return pltpu.make_async_remote_copy(
            src_ref=packed.at[first_head(target) + slot],
            dst_ref=place(slot, me),
            send_sem=kv_send.at[slot, target],
            recv_sem=kv_recv.at[slot, me],
            device_id={"patch": target},
            device_id_type=MESH,
        )

    my_first = first_head(me)
    my_last = last_head(me)

    def pack_kv(step, unused):
        lanes = pl.ds(pl.multiple_of(step * LANES, LANES), LANES)
        keys = stale[0, :, lanes].astype(F32)
        values = stale[1, :, lanes].astype(F32)
        mask = half_mask(block)
        packed[2 * step] = jnp.where(mask, keys, swap(values)).astype(BF16)
        packed[2 * step + 1] = jnp.where(mask, swap(keys), values).astype(BF16)
        return unused

    stale_load.wait()
    lax.fori_loop(0, pairs, pack_kv, 0)
    for slot in range(slots):

        @pl.when(my_first + slot <= my_last)
        def _():
            kvs[slot, pl.ds(pl.multiple_of(me * block, block), block), :] = packed[my_first + slot]


    loads[0].wait()

    @pl.when(me == 0)
    def _():
        feat[0:cols, :] = jnp.zeros((cols, width_in), BF16)

    @pl.when(me == size - 1)
    def _():
        feat[block + cols : block + 2 * cols, :] = jnp.zeros((cols, width_in), BF16)

    def sum_rows(step, carry):
        first, second = carry
        x = feat[pl.ds(pl.multiple_of(cols + step * 16, 16), 16), :].astype(F32)
        low, high = x[:8], x[8:]
        return first + (low + high), second + (low * low + high * high)

    zero = jnp.zeros((8, width_in), F32)
    first, second = lax.fori_loop(0, block // 16, sum_rows, (zero, zero))
    sums = two_rows(
        jnp.sum(first, axis=0, keepdims=True), jnp.sum(second, axis=0, keepdims=True)
    )
    stat_out1[...] = group_sums(sums)
    pl.semaphore_wait(barrier, size - 1)

    def stat_copy(which, out, into, target, index):
        return pltpu.make_async_remote_copy(
            src_ref=out,
            dst_ref=into.at[me],
            send_sem=stat_send.at[which, target],
            recv_sem=stat_recv.at[which, index],
            device_id={"patch": target},
            device_id_type=MESH,
        )

    def stats_start(which, out, into):
        def send(step, unused):
            target = lax.rem(me + step, size)
            stat_copy(which, out, into, target, me).start()
            return unused

        lax.fori_loop(1, size, send, 0)

    def stats_finish(which, out, into):
        def receive(step, total):
            source = lax.rem(me + step, size)
            pltpu.make_async_remote_copy(
                src_ref=out,
                dst_ref=into.at[source],
                send_sem=stat_send.at[which, source],
                recv_sem=stat_recv.at[which, source],
                device_id={"patch": source},
                device_id_type=MESH,
            ).wait()
            return total + into[source]

        return lax.fori_loop(1, size, receive, out[...])

    stats_start(0, stat_out1, stat_in1)

    top_row = feat.at[pl.ds(cols, cols), :]
    bottom_row = feat.at[pl.ds(block, cols), :]
    above = feat.at[pl.ds(0, cols), :]
    below = feat.at[pl.ds(block + cols, cols), :]
    up = pltpu.make_async_remote_copy(
        src_ref=top_row,
        dst_ref=below,
        send_sem=halo_send.at[0],
        recv_sem=halo_recv.at[0],
        device_id={"patch": lax.rem(me + size - 1, size)},
        device_id_type=MESH,
    )
    down = pltpu.make_async_remote_copy(
        src_ref=bottom_row,
        dst_ref=above,
        send_sem=halo_send.at[1],
        recv_sem=halo_recv.at[1],
        device_id={"patch": lax.rem(me + 1, size)},
        device_id_type=MESH,
    )

    @pl.when(me > 0)
    def _():
        up.start()

    @pl.when(me < size - 1)
    def _():
        down.start()

    def send_kv(step, unused):
        target = lax.rem(me + step, size)
        kv_copy(0, target).start()
        for slot in range(1, slots):

            @pl.when(first_head(target) + slot <= last_head(target))
            def _():
                kv_copy(slot, target).start()

        return unused

    lax.fori_loop(1, size, send_kv, 0)

    loads[1].wait()
    mixed[...] = dot(feat[inside, :], shortw[...]) + dot(embed_ref[...], time_ref[...])[0:1]

    total = stats_finish(0, stat_out1, stat_in1)
    count = float(size * block * (width_in // GROUPS))
    center, inverse = group_stats(total, count, width_in, 1e-05)
    scale = inverse * gain_one_ref[...].reshape(1, width_in)

    @pl.when(me > 0)
    def _():
        up.wait_send()
        down.wait_recv()

    @pl.when(me < size - 1)
    def _():
        down.wait_send()
        up.wait_recv()

    def activate(step, unused):
        x = feat[pl.ds(pl.multiple_of(step * 16, 16), 16), :].astype(F32)
        y = (x - center) * scale
        half = 0.5 * y
        z = half + half * jnp.tanh(half)
        act[pl.ds(pl.multiple_of(step * 16, 16), 16), :] = z.astype(BF16)
        return unused

    lax.fori_loop(0, act.shape[0] // 16, activate, 0)

    @pl.when(me == 0)
    def _():
        act[0:cols, :] = jnp.zeros((cols, width_in), BF16)

    @pl.when(me == size - 1)
    def _():
        act[block + cols : block + 2 * cols, :] = jnp.zeros((cols, width_in), BF16)

    for dx in range(3):
        conv_loads[1][dx].wait()

    def middle(dx, unused):
        parts[dx] = dot(act[pl.ds(cols, block), :], convw[1, dx])
        return unused

    lax.fori_loop(0, 3, middle, 0)

    for dy in (0, 2):
        for dx in range(3):
            conv_loads[dy][dx].wait()

    def outer(dx, unused):
        parts[dx] = (
            parts[dx]
            + dot(act[pl.ds(0, block), :], convw[0, dx])
            + dot(act[pl.ds(2 * cols, block), :], convw[2, dx])
        )
        return unused

    lax.fori_loop(0, 3, outer, 0)

    col = lax.rem(lax.broadcasted_iota(jnp.int32, (block, LANES), 0), cols)
    sums = []
    for pair in range(pairs):
        lanes = pl.ds(pair * LANES, LANES)
        left = jnp.where(col == 0, 0.0, pltpu.roll(parts[0, :, lanes], 1, 0))
        right = jnp.where(col == cols - 1, 0.0, pltpu.roll(parts[2, :, lanes], block - 1, 0))
        value = mixed[:, lanes] + (left + parts[1, :, lanes] + right)
        mixed[:, lanes] = value
        sums.append(
            two_rows(
                jnp.sum(value, axis=0, keepdims=True),
                jnp.sum(value * value, axis=0, keepdims=True),
            )
        )
    stat_out2[...] = group_sums(jnp.concatenate(sums, axis=1))
    stats_start(1, stat_out2, stat_in2)
    for load in loads[2:]:
        load.wait()
    total = stats_finish(1, stat_out2, stat_in2)
    count = float(size * block * (width // GROUPS))
    center, inverse = group_stats(total, count, width, 1e-06)
    normed = ((mixed[...] - center) * (inverse * gain_two_ref[...].reshape(1, width))).astype(BF16)

    def task_of(head):
        task = head * size + me
        return lax.div(task, heads), lax.rem(task, heads)

    def q_remote(head, target, slot):
        return pltpu.make_async_remote_copy(
            src_ref=q_out.at[head],
            dst_ref=q_in.at[slot],
            send_sem=q_send.at[head],
            recv_sem=q_recv.at[slot],
            device_id={"patch": target},
            device_id_type=MESH,
        )

    queries = dot(normed, projw[0]).astype(BF16)
    for pair in range(pairs):
        both = queries[:, pair * LANES : (pair + 1) * LANES]
        fresh[0, pair] = both
        q_out[2 * pair] = fold(both, 0)
        q_out[2 * pair + 1] = fold(both, 1)

    def send_queries(head, unused):
        target, slot = task_of(head)

        @pl.when(target != me)
        def _():
            q_remote(head, target, slot).start()

        @pl.when(target == me)
        def _():
            pltpu.make_async_copy(q_out.at[head], q_in.at[slot], q_recv.at[slot]).start()

        return unused

    lax.fori_loop(0, heads, send_queries, 0)

    for kind in (1, 2):
        value = dot(normed, projw[kind]).astype(BF16)
        for pair in range(pairs):
            fresh[kind, pair] = value[:, pair * LANES : (pair + 1) * LANES]

    left_half = half_mask(block)
    ones = jnp.ones((block, LANES), BF16)

    def heads_of(query):
        none = jnp.zeros_like(query)
        return jnp.where(left_half, query, none), jnp.where(left_half, none, query)

    def finish(pieces):
        values, lses = [], []
        for summed, height in pieces:
            weight = summed[:, LANES:]
            values.append(summed[:, :LANES] / weight)
            lses.append(height * 0.125 + jnp.log(weight))
        return jnp.where(left_half, *values), jnp.where(left_half, *lses)

    def own_attention(pair, unused):
        keys = fresh[1, pair]
        values = jnp.concatenate([fresh[2, pair], ones], axis=1)
        pieces = []
        for query in heads_of(fresh[0, pair]):
            scores = scores_of(query, keys)
            height = jnp.max(scores, axis=1, keepdims=True)
            weights = jnp.exp2((scores - height) * EXP_SCALE).astype(BF16)
            pieces.append((dot(weights, values), jnp.broadcast_to(height, (block, LANES))))
        own_val[pair], own_lse[pair] = finish(pieces)
        return unused

    lax.fori_loop(0, pairs, own_attention, 0)

    def kv_wait(slot, source):
        pltpu.make_async_remote_copy(
            src_ref=place(slot, source),
            dst_ref=place(slot, source),
            send_sem=kv_send.at[slot, source],
            recv_sem=kv_recv.at[slot, source],
            device_id={"patch": source},
            device_id_type=MESH,
        ).wait_recv()

    def receive_kv(step, unused):
        source = lax.rem(me + step, size)
        kv_wait(0, source)
        for slot in range(1, slots):

            @pl.when(my_first + slot <= my_last)
            def _():
                kv_wait(slot, source)

        return unused

    lax.fori_loop(1, size, receive_kv, 0)

    def place_of(index):
        task = me * heads + index
        return lax.div(task, size), lax.rem(task, size)

    def unfold(x):
        mask = half_mask(block // 2)
        upper = jnp.where(mask, x.astype(F32), 0.0)
        lower = jnp.where(mask, swap(x), 0.0)
        return jnp.concatenate([upper, lower], axis=0).astype(BF16)

    fill = jnp.where(half_mask(1), 1.0, 0.0).astype(BF16)
    keep = jnp.where(half_mask(1), 0.0, 1.0).astype(BF16)

    def run_tasks(couple, unused):
        tasks = []
        for which in range(2):
            index = 2 * couple + which
            head, owner = place_of(index)
            pltpu.make_async_copy(q_in.at[index], q_in.at[index], q_recv.at[index]).wait()
            tasks.append((head - my_first, owner, unfold(q_in[index])))

        def partial(slot, owner, step):
            rows = pl.ds(pl.multiple_of(lax.rem(owner + step, size) * block, block), block)
            both = kvs[slot, rows, :]
            return both, both * keep + fill

        for which, (slot, owner, query) in enumerate(tasks):
            keys, values = partial(slot, owner, 1)
            scores = scores_of(query, keys)
            height = jnp.max(scores, axis=1, keepdims=True)
            weights = jnp.exp2((scores - height) * EXP_SCALE).astype(BF16)
            acc[which] = dot(weights, values)
            top[which] = jnp.broadcast_to(height, (block, LANES))

        def more(step, unused):
            for which, (slot, owner, query) in enumerate(tasks):
                keys, values = partial(slot, owner, step)
                scores = scores_of(query, keys)
                before = top[which]
                height = jnp.maximum(before, jnp.max(scores, axis=1, keepdims=True))
                factor = jnp.exp2((before - height) * EXP_SCALE)
                weights = jnp.exp2((scores - height[:, :1]) * EXP_SCALE).astype(BF16)
                acc[which] = acc[which] * factor + dot(weights, values)
                top[which] = height
            return unused

        lax.fori_loop(2, size, more, 0)
        lses = []
        for which in range(2):
            index = 2 * couple + which
            summed = acc[which]
            total = swap(summed)
            res[index] = fold(summed / total, 1)
            lses.append(top[which] * 0.125 + jnp.log(total))
        turned = jnp.transpose(jnp.where(left_half, swap(lses[0]), lses[1]))
        res_lse[2 * couple] = turned[0:8]
        res_lse[2 * couple + 1] = turned[HEAD_DIM : HEAD_DIM + 8]
        for which in range(2):
            index = 2 * couple + which
            head, owner = place_of(index)

            @pl.when(owner != me)
            def _():
                for copy in result_copies(index, head, owner):
                    copy.start()

            @pl.when(owner == me)
            def _():
                pltpu.make_async_copy(res.at[index], res_in.at[head], res_recv.at[head]).start()
                pltpu.make_async_copy(
                    res_lse.at[index], lse_in.at[head], lse_recv.at[head]
                ).start()

        return unused

    def result_copies(index, head, owner):
        return [
            pltpu.make_async_remote_copy(
                src_ref=source.at[index],
                dst_ref=into.at[head],
                send_sem=sent.at[index],
                recv_sem=received.at[head],
                device_id={"patch": owner},
                device_id_type=MESH,
            )
            for source, into, sent, received in (
                (res, res_in, res_send, res_recv),
                (res_lse, lse_in, lse_send, lse_recv),
            )
        ]

    lax.fori_loop(0, pairs, run_tasks, 0)

    output = mixed[...]
    for pair in range(heads):
        pltpu.make_async_copy(res_in.at[pair], res_in.at[pair], res_recv.at[pair]).wait()
        pltpu.make_async_copy(lse_in.at[pair], lse_in.at[pair], lse_recv.at[pair]).wait()
    merged = []
    for pair in range(pairs):
        rows = lax.broadcasted_iota(jnp.int32, (LANES, block), 0) < HEAD_DIM
        lse = jnp.transpose(jnp.where(rows, lse_in[2 * pair, 0:1], lse_in[2 * pair + 1, 0:1]))
        mine = own_lse[pair]
        best = jnp.maximum(lse, mine)
        there = jnp.exp(lse - best)
        here = jnp.exp(mine - best)
        first, second = res_in[2 * pair].astype(F32), res_in[2 * pair + 1].astype(F32)
        mask = half_mask(block // 2)
        upper = jnp.where(mask, first, swap(second))
        lower = jnp.where(mask, swap(first), second)
        value = (there * jnp.concatenate([upper, lower], axis=0) + here * own_val[pair]) / (there + here)
        merged.append(value.astype(BF16))
    out_ref[...] = (output + dot(jnp.concatenate(merged, axis=1), projw[3])).astype(BF16)

    def sent_kv(step, unused):
        target = lax.rem(me + step, size)
        kv_copy(0, target).wait_send()
        for slot in range(1, slots):

            @pl.when(first_head(target) + slot <= last_head(target))
            def _():
                kv_copy(slot, target).wait_send()

        return unused

    lax.fori_loop(1, size, sent_kv, 0)

    def sent_rest(index, unused):
        target, slot = task_of(index)

        @pl.when(target != me)
        def _():
            q_remote(index, target, slot).wait_send()

        head, owner = place_of(index)

        @pl.when(owner != me)
        def _():
            for copy in result_copies(index, head, owner):
                copy.wait_send()

        return unused

    lax.fori_loop(0, heads, sent_rest, 0)


def slots_for(heads, size):
    return max(
        (device * heads + heads - 1) // size - device * heads // size + 1
        for device in range(size)
    )


def on_device(
    features,
    stale_kv,
    timestep,
    time_w,
    gain_one,
    conv_w,
    shortcut_w,
    gain_two,
    query_w,
    key_w,
    value_w,
    out_w,
):
    rows, cols, width_in = features.shape
    width = shortcut_w.shape[1]
    block = rows * cols
    size = lax.axis_size("patch")
    pairs = width // LANES
    heads = width // HEAD_DIM
    half = FREQ // 2
    freqs = jnp.exp(-math.log(10000.0) * jnp.arange(half, dtype=F32) / half)
    angles = timestep.astype(F32)[0] * freqs
    embed = jnp.concatenate([jnp.cos(angles), jnp.sin(angles)]).astype(BF16)
    embed = jnp.broadcast_to(embed[None, :], (16, FREQ))
    anywhere = pl.BlockSpec(memory_space=pl.ANY)
    vmem = pl.BlockSpec(memory_space=pltpu.VMEM)
    dma = pltpu.SemaphoreType.DMA
    flops = 2 * block * width * (10 * width_in + 4 * width + 4 * size * block)
    output = pl.pallas_call(
        functools.partial(fused_kernel, size),
        out_shape=jax.ShapeDtypeStruct((block, width), BF16),
        in_specs=[anywhere, anywhere, vmem, vmem, vmem, anywhere, anywhere, vmem]
        + [anywhere] * 4,
        out_specs=vmem,
        scratch_shapes=[
            pltpu.VMEM((block + 2 * cols, width_in), BF16),
            pltpu.VMEM((3, 3, width_in, width), BF16),
            pltpu.VMEM((width_in, width), BF16),
            pltpu.VMEM((4, width, width), BF16),
            pltpu.VMEM((block + 2 * cols, width_in), BF16),
            pltpu.VMEM((3, block, width), F32),
            pltpu.VMEM((block, width), F32),
            pltpu.VMEM((slots_for(heads, size), size * block, LANES), BF16),
            pltpu.VMEM((2, block, width), BF16),
            pltpu.VMEM((heads, block, LANES), BF16),
            pltpu.VMEM((8, LANES), F32),
            pltpu.VMEM((size, 8, LANES), F32),
            pltpu.VMEM((8, LANES), F32),
            pltpu.VMEM((size, 8, LANES), F32),
            pltpu.VMEM((3, pairs, block, LANES), BF16),
            pltpu.VMEM((heads, block // 2, LANES), BF16),
            pltpu.VMEM((heads, block // 2, LANES), BF16),
            pltpu.VMEM((pairs, block, LANES), F32),
            pltpu.VMEM((pairs, block, LANES), F32),
            pltpu.VMEM((2, block, LANES), F32),
            pltpu.VMEM((2, block, LANES), F32),
            pltpu.VMEM((heads, block // 2, LANES), BF16),
            pltpu.VMEM((heads, 8, block), F32),
            pltpu.VMEM((heads, block // 2, LANES), BF16),
            pltpu.VMEM((heads, 8, block), F32),
            dma((7,)),
            dma((3, 3)),
            dma((slots_for(heads, size), size)),
            dma((slots_for(heads, size), size)),
            dma((2, size)),
            dma((2, size)),
            dma((2,)),
            dma((2,)),
            dma((heads,)),
            dma((heads,)),
            dma((heads,)),
            dma((heads,)),
            dma((heads,)),
            dma((heads,)),
        ],
        compiler_params=pltpu.CompilerParams(
            collective_id=0, has_side_effects=True, vmem_limit_bytes=58 * 1024 * 1024
        ),
        cost_estimate=pl.CostEstimate(
            flops=flops, bytes_accessed=24_000_000, transcendentals=block * size * block * 10
        ),
    )(
        stale_kv,
        features.reshape(block, width_in),
        embed,
        time_w,
        gain_one,
        conv_w,
        shortcut_w,
        gain_two,
        query_w,
        key_w,
        value_w,
        out_w,
    )
    return output.reshape(rows, cols, width)


def solution(mesh):
    return jax.shard_map(
        on_device,
        mesh=mesh,
        in_specs=(
            P("patch", "batch", None),
            P("batch", "patch", None),
            P("batch"),
            P(),
            P(),
            P(),
            P(),
            P(),
            P(),
            P(),
            P(),
            P(),
        ),
        out_specs=P("patch", "batch", None),
        check_vma=False,
    )
```
